32 devices in a mesh: groups: 2 (over x), row: 16 (over z, y, core).
Axes of the slice: x: 2, y: 2, z: 4, core: 2. Of those that a mesh axis runs over, the one named last changes fastest.
Arguments:
- head_out: bfloat16 [16, 1536, 1024], P('row', 'groups'), parts along dimension 1, may hold values from -6 to 6
- out_grad: bfloat16 [16, 1536, 1024], P('row', 'groups'), parts along dimension 1, may hold values from -6 to 6
- proj_weight: bfloat16 [16, 1024, 1024], P('row'), may hold values from -0.09375 to 0.09375
Outputs:
- projected: bfloat16 [16, 1536, 1024], P('row', 'groups'), parts along dimension 1
- head_grad: bfloat16 [16, 1536, 1024], P('row', 'groups'), parts along dimension 1
The draws below stay inside these ranges and needn't reach their ends.
There are 2 independent parts, one for each index of `groups`. The reference program is written for one: setup_inputs(seed, part) draws one part's arguments, and reference() takes and returns one part's arrays. A program takes and returns all parts, laid end to end along the dimension named above; an argument that names none is the same for every part. Nothing has to cross between parts.
All inputs are finite; a program needn't handle non-finite values.
Results may differ from the reference program's by a relative error of at most 0.001.
Values may be sent and summed in bfloat16 or wider, within the bound.
No kernel may reach another device: no remote copies, remote signals or barrier semaphores. Data moves between devices by JAX's collectives and lax.ppermute only.
A program may use at most 128 MiB of HBM per device.

```python
import jax
import jax.numpy as jnp

D_IN = 4096
TOK_BLOCK = 768
GRID = 4
IN_BLOCK = 1024
OUT_BLOCK = 1024
N_ROW = 16


def block_scale(key, extent, cuts, low, top_value):
    gain = 1.0
    for dim, parts in cuts:
        draws = jax.random.uniform(jax.random.fold_in(jax.random.fold_in(key, 6), dim), (parts,), jnp.float32, low / len(cuts), top_value / len(cuts))
        gain = gain * jnp.repeat(jnp.exp(draws), extent[dim] // parts).reshape((-1,) + (1,) * (len(extent) - 1 - dim))
    return gain


def scatter_about(own_key, extent, spread, most, pieces=(), kind=jnp.bfloat16):
    gain = block_scale(own_key, extent, pieces, -0.22, 0.18) if pieces else 1.0
    result = jax.random.normal(own_key, extent, jnp.float32) * spread * gain
    return jnp.minimum(jnp.maximum(result, -most), most).astype(kind)


def setup_inputs(seed: int = 0, part: int = 0) -> dict:
    keys = jax.random.split(jax.random.key(seed), 4)
    part_splits = jax.random.split(jax.random.fold_in(keys[3], part), 4)
    head_out = scatter_about(part_splits[0], (N_ROW, TOK_BLOCK, IN_BLOCK), 1.0, 6.0, ((0, 16),))
    out_grad = scatter_about(part_splits[1], (N_ROW, TOK_BLOCK, OUT_BLOCK), 1.0, 6.0, ((0, 16),))
    proj_weight = scatter_about(keys[2], (N_ROW, IN_BLOCK, OUT_BLOCK), D_IN ** -0.5, 0.09375, ((0, 16),))
    return dict(head_out=head_out, out_grad=out_grad, proj_weight=proj_weight)


def blocks_to_whole(blocks, rows, cols):
    return blocks.reshape(GRID, GRID, rows, cols).transpose(0, 2, 1, 3).reshape(GRID * rows, GRID * cols)


def whole_to_blocks(whole, rows, cols):
    return whole.reshape(GRID, rows, GRID, cols).transpose(0, 2, 1, 3).reshape(GRID * GRID, rows, cols)


def reference(head_out, out_grad, proj_weight):
    head_whole = blocks_to_whole(head_out, TOK_BLOCK, IN_BLOCK)
    cotangent_whole = blocks_to_whole(out_grad, TOK_BLOCK, OUT_BLOCK)
    weight_whole = blocks_to_whole(proj_weight, IN_BLOCK, OUT_BLOCK)
    forward = jnp.dot(head_whole, weight_whole, preferred_element_type=jnp.float32).astype(jnp.bfloat16)
    backward = jnp.dot(cotangent_whole, weight_whole.T, preferred_element_type=jnp.float32).astype(jnp.bfloat16)
    projected = whole_to_blocks(forward, TOK_BLOCK, OUT_BLOCK)
    head_grad = whole_to_blocks(backward, TOK_BLOCK, IN_BLOCK)
    return projected, head_grad
```

```python
import jax
import jax.numpy as jnp
from jax import lax
from jax.sharding import Mesh
from jax.sharding import PartitionSpec as P


def partner_2(value, axis, distance):
    return lax.ppermute(value, axis, [(i, i ^ 1 << distance) for i in range(lax.axis_size(axis))])


def bit_at(device_index, position):
    return jnp.bitwise_and(jnp.right_shift(device_index, position), 1)


def grow_panel(own_block, bit_order, offset, device_index):
    panel = own_block
    for level_bit in bit_order:
        own_bit = bit_at(device_index, offset + level_bit)
        partner = partner_2(panel, "row", offset + level_bit)
        low_part = jnp.where(own_bit == 0, panel, partner)
        high_part = jnp.where(own_bit == 0, partner, panel)
        panel = jnp.stack([low_part, high_part], 0)
    return panel


def turn_panel(panel, layout, device_index, bit_order):
    for level_bit in bit_order:
        axis_at = layout.index(level_bit)
        own_bit = bit_at(device_index, level_bit)
        kept_half = lax.dynamic_index_in_dim(panel, own_bit, axis_at, keepdims=False)
        sent_half = lax.dynamic_index_in_dim(panel, 1 - own_bit, axis_at, keepdims=False)
        partner = partner_2(sent_half, "row", level_bit)
        low_part = jnp.where(own_bit == 0, kept_half, partner)
        high_part = jnp.where(own_bit == 0, partner, kept_half)
        panel = jnp.stack([low_part, high_part], axis_at)
    return panel


def any_grid(head_out, out_grad, proj_weight):
    levels = (lax.axis_size("row").bit_length() - 1) // 2
    device_index = lax.axis_index("row")
    bit_order = list(range(levels))
    layout = bit_order[::-1]
    letters = "pqrsuv"[:levels]
    head_panel = grow_panel(head_out[0], bit_order, 0, device_index)
    weight_panel = grow_panel(proj_weight[0], bit_order, levels, device_index)
    forward = jnp.einsum(
        letters + "ti," + letters + "io->to", head_panel, weight_panel, preferred_element_type=jnp.float32
    )
    turned = turn_panel(weight_panel, layout, device_index, bit_order)
    grad_panel = grow_panel(out_grad[0], bit_order, 0, device_index)
    summed = jnp.einsum(
        letters + "to," + letters + "io->ti", grad_panel, turned, preferred_element_type=jnp.float32
    )
    return forward.astype(jnp.bfloat16)[None], summed.astype(jnp.bfloat16)[None]


def swap(value, axis):
    return lax.ppermute(value, axis, [(0, 1), (1, 0)])


def send(value, pairs):
    return lax.ppermute(value, "a", pairs)


def pick(flag, yes, no):
    return jnp.where(flag, yes, no)


def two_of(flag, first, second):
    return pick(flag == 0, first, second), pick(flag == 0, second, first)


def rows_times(left, right):
    return lax.dot_general(left, right, (((1,), (1,)), ((), ())), preferred_element_type=jnp.float32)


def times(left, right):
    return lax.dot_general(left, right, (((1,), (0,)), ((), ())), preferred_element_type=jnp.float32)


def grid_4(head_out, out_grad, proj_weight):
    group = lax.axis_index("g")
    plane = lax.axis_index("a")
    chip = lax.axis_index("b")
    core = lax.axis_index("k")
    tokens, features = head_out.shape[1:]
    half, quarter = features // 2, features // 4

    weight = proj_weight[0].reshape(2, 2, quarter, -1)
    kept = lax.dynamic_index_in_dim(weight, core, 0, keepdims=False)
    given = lax.dynamic_index_in_dim(weight, 1 - core, 0, keepdims=False)
    own_row = jnp.stack([kept, swap(given, "k")], 0)
    mine = lax.dynamic_index_in_dim(own_row, group, 1, keepdims=False)
    other = lax.dynamic_index_in_dim(own_row, 1 - group, 1, keepdims=False)

    heads = head_out[0].reshape(tokens, 2, half)
    head_kept = lax.dynamic_index_in_dim(heads, core, 1, keepdims=False)
    head_given = lax.dynamic_index_in_dim(heads, 1 - core, 1, keepdims=False)
    head_pair = jnp.stack([head_kept, swap(head_given, "k")], 0)
    head_far = swap(head_pair, "b")
    grad_0 = out_grad[0]
    grad_1 = swap(grad_0, "k")

    is_mid = (plane == 1) | (plane == 2)
    near_a = send(mine, [(0, 1), (1, 0), (2, 3), (3, 2)])
    middle = send(mine, [(1, 2), (2, 1)])
    end_1 = send(middle, [(1, 0), (2, 3)])
    cross = send(near_a, [(1, 2), (2, 1)])
    end_2 = send(cross, [(1, 0), (2, 3)])
    far_1 = pick(is_mid, middle, end_1)
    far_2 = pick(is_mid, cross, end_2)
    near_x = swap(near_a, "g")
    far_1x = swap(far_1, "g")
    far_2x = swap(far_2, "g")

    def back(piece):
        return rows_times(grad_0, piece[0]) + rows_times(grad_1, piece[1])

    early = plane // 2 != chip

    def exchange(near_piece, far_piece):
        near_sum, far_sum = back(near_piece), back(far_piece)
        there = swap(pick(early, near_sum, far_sum), "b")
        return (pick(early, far_sum, near_sum) + there).astype(jnp.bfloat16)

    grads_z = exchange(mine, far_1), exchange(near_a, far_2)
    grads_x = exchange(other, far_1x), exchange(near_x, far_2x)
    first = jnp.stack(two_of(group, grads_z[0], grads_x[0]), 1)
    second = jnp.stack(two_of(group, grads_z[1], grads_x[1]), 1)
    parity = pick(early, plane // 2, plane & 1)
    mine_out, theirs_out = two_of(parity ^ core, first, second)
    got = swap(theirs_out, "k")
    low, high = two_of(core, mine_out, got)
    head_grad = jnp.concatenate([low.reshape(tokens, half), high.reshape(tokens, half)], 1)

    head_all = jnp.concatenate([head_pair, head_far], 0).reshape(4, tokens, 2, quarter)

    def head_of(row, of_group):
        slot = 2 * (row // 2 != chip) + ((row & 1) != core)
        return head_all[slot, :, of_group]

    low_plane = plane < 2
    rows = [plane, plane ^ 1, pick(low_plane, 2, 1), pick(low_plane, 3, 0)]
    pieces_z = [mine, near_a, far_1, far_2]
    pieces_x = [other, near_x, far_1x, far_2x]
    lhs = jnp.concatenate([head_of(r, group) for r in rows] + [head_of(r, 1 - group) for r in rows], 1)
    totals = [
        times(lhs, jnp.concatenate([piece[slot] for piece in pieces_z + pieces_x], 0)) for slot in (0, 1)
    ]
    projected = (totals[0] + swap(totals[1], "k")).astype(jnp.bfloat16)
    return projected[None], head_grad[None]


def solution(mesh):
    n_group, n_row = mesh.shape["groups"], mesh.shape["row"]
    if (n_group, n_row) == (2, 16):
        grid = Mesh(mesh.devices.reshape(2, 4, 2, 2), ("g", "a", "b", "k"))
        tokens, whole = P(("a", "b", "k"), "g", None), P(("a", "b", "k"), None, None)
        body = grid_4
    else:
        grid = mesh
        tokens, whole = P("row", "groups", None), P("row", None, None)
        body = any_grid
    return jax.shard_map(
        body, mesh=grid, in_specs=(tokens, tokens, whole), out_specs=(tokens, tokens), check_vma=False
    )
```

```python
import functools

import jax
import jax.numpy as jnp
from jax import lax
from jax.experimental import pallas as pl
from jax.experimental.pallas import tpu as pltpu
from jax.sharding import Mesh
from jax.sharding import PartitionSpec as P


def partner_2(value, axis, distance):
    return lax.ppermute(value, axis, [(i, i ^ 1 << distance) for i in range(lax.axis_size(axis))])


def bit_at(device_index, position):
    return jnp.bitwise_and(jnp.right_shift(device_index, position), 1)


def grow_panel(own_block, bit_order, offset, device_index):
    panel = own_block
    for level_bit in bit_order:
        own_bit = bit_at(device_index, offset + level_bit)
        partner = partner_2(panel, "row", offset + level_bit)
        low_part = jnp.where(own_bit == 0, panel, partner)
        high_part = jnp.where(own_bit == 0, partner, panel)
        panel = jnp.stack([low_part, high_part], 0)
    return panel


def turn_panel(panel, layout, device_index, bit_order):
    for level_bit in bit_order:
        axis_at = layout.index(level_bit)
        own_bit = bit_at(device_index, level_bit)
        kept_half = lax.dynamic_index_in_dim(panel, own_bit, axis_at, keepdims=False)
        sent_half = lax.dynamic_index_in_dim(panel, 1 - own_bit, axis_at, keepdims=False)
        partner = partner_2(sent_half, "row", level_bit)
        low_part = jnp.where(own_bit == 0, kept_half, partner)
        high_part = jnp.where(own_bit == 0, partner, kept_half)
        panel = jnp.stack([low_part, high_part], axis_at)
    return panel


def any_grid(head_out, out_grad, proj_weight):
    levels = (lax.axis_size("row").bit_length() - 1) // 2
    device_index = lax.axis_index("row")
    bit_order = list(range(levels))
    layout = bit_order[::-1]
    letters = "pqrsuv"[:levels]
    head_panel = grow_panel(head_out[0], bit_order, 0, device_index)
    weight_panel = grow_panel(proj_weight[0], bit_order, levels, device_index)
    forward = jnp.einsum(
        letters + "ti," + letters + "io->to", head_panel, weight_panel, preferred_element_type=jnp.float32
    )
    turned = turn_panel(weight_panel, layout, device_index, bit_order)
    grad_panel = grow_panel(out_grad[0], bit_order, 0, device_index)
    summed = jnp.einsum(
        letters + "to," + letters + "io->ti", grad_panel, turned, preferred_element_type=jnp.float32
    )
    return forward.astype(jnp.bfloat16)[None], summed.astype(jnp.bfloat16)[None]


def swap(value, axis):
    return lax.ppermute(value, axis, [(0, 1), (1, 0)])


def send(value, pairs):
    return lax.ppermute(value, "a", pairs)


def after(value, *earlier):
    return lax.optimization_barrier((value, *earlier))[0]


def pick(flag, yes, no):
    return jnp.where(flag, yes, no)


def times(left, right):
    return lax.dot_general(left, right, (((1,), (0,)), ((), ())), preferred_element_type=jnp.float32)


def times_rows(left, right):
    return lax.dot_general(left, right, (((1,), (1,)), ((), ())), preferred_element_type=jnp.float32)


def sum_of_products(n_base, numbers, *refs):
    heads, base, pieces, out = refs[:4], refs[4 : 4 + n_base], refs[4 + n_base : -1], refs[-1]
    quarter = pieces[0].shape[0]
    total = None
    for term, piece in enumerate(pieces):
        slot, side = numbers[1 + 2 * term], numbers[2 + 2 * term]
        head = heads[3][...]
        for other in (2, 1, 0):
            head = jnp.where(slot == other, heads[other][...], head)
        head = jnp.where(side == 0, head[:, :quarter], head[:, quarter:])
        product = times(head, piece[...])
        total = product if total is None else total + product
    for term in base:
        total = total + term[...]
    out[...] = total.astype(out.dtype)


def forward_sum(numbers, heads, base, pieces, dtype):
    tokens, width = heads[0].shape
    tile = tokens // 2
    by_rows = pl.BlockSpec((tile, width), lambda i, _: (i, 0))
    spec = pltpu.PrefetchScalarGridSpec(
        num_scalar_prefetch=1,
        grid=(tokens // tile,),
        in_specs=[pl.BlockSpec((tile, width // 2), lambda i, numbers: (i, numbers[0]))] * 4
        + [by_rows] * len(base)
        + [pl.BlockSpec(p.shape, lambda i, _: (0, 0)) for p in pieces],
        out_specs=by_rows,
    )
    return pl.pallas_call(
        functools.partial(sum_of_products, len(base)),
        grid_spec=spec,
        out_shape=jax.ShapeDtypeStruct((tokens, width), dtype),
        compiler_params=pltpu.CompilerParams(
            dimension_semantics=("arbitrary",), vmem_limit_bytes=26 * 1024 * 1024
        ),
        cost_estimate=pl.CostEstimate(flops=1000, bytes_accessed=1000, transcendentals=0),
    )(jnp.stack(numbers).astype(jnp.int32), *heads, *base, *pieces)


INWARD = [(0, 1), (3, 2)]
MIDDLE = [(1, 2), (2, 1)]
OUTWARD = [(1, 0), (2, 3)]
BOTH = INWARD + OUTWARD


def grid_4(head_out, out_grad, proj_weight):
    group = lax.axis_index("g")
    plane = lax.axis_index("a")
    chip = lax.axis_index("b")
    core = lax.axis_index("k")
    heads, grad_0, weight = head_out[0], out_grad[0], proj_weight[0]
    tokens, width = heads.shape
    half, quarter = width // 2, width // 4
    is_mid = (plane == 1) | (plane == 2)
    early = plane // 2 != chip

    def weight_rows(block, of_core, of_group):
        return lax.dynamic_slice_in_dim(block, of_core * half + of_group * quarter, quarter, 0)

    mine_0 = weight_rows(weight, core, group)
    middle_0 = send(mine_0, MIDDLE)
    mine_1 = swap(weight_rows(after(weight, mine_0), 1 - core, group), "k")
    head_y = swap(heads, "b")
    near_1 = send(mine_1, BOTH)
    middle_1 = send(after(mine_1, middle_0), MIDDLE)
    grad_1 = swap(grad_0, "k")
    x_1 = swap(near_1, "g")
    ahead = is_mid & jnp.logical_not(early)
    out_2 = send(pick(ahead, middle_0, after(mine_0, near_1)), BOTH)
    cross_1 = send(after(near_1, middle_1), MIDDLE)
    mid_3 = pick(early, middle_0, after(middle_1, near_1))
    at_2 = pick(ahead, middle_0, out_2)
    out_3 = send(after(mid_3, out_2), OUTWARD)
    x_2 = swap(after(at_2, x_1, grad_1, head_y), "g")
    cross_0 = send(after(out_2, cross_1), MIDDLE)
    late_weight = after(weight, x_1)
    other_0 = weight_rows(late_weight, core, 1 - group)
    other_1 = swap(weight_rows(late_weight, 1 - core, 1 - group), "k")
    mid_4 = pick(early, middle_1, after(cross_1, out_3))
    out_4 = send(mid_4, OUTWARD)
    at_3 = pick(is_mid, mid_3, after(out_3, x_1))
    x_3 = swap(after(at_3, x_2), "g")
    mid_5 = pick(early, cross_1, after(cross_0, out_4))
    out_5 = send(mid_5, OUTWARD)
    at_4 = pick(is_mid, mid_4, after(out_4, x_2))
    x_4 = swap(after(at_4, x_3, other_1), "g")
    out_6 = send(pick(early, cross_0, after(mine_0, out_5)), OUTWARD)
    at_5 = pick(is_mid, mid_5, after(out_5, x_3))
    x_5 = swap(after(at_5, x_4), "g")
    at_6 = pick(is_mid, pick(early, cross_0, out_2), after(out_6, x_4))
    x_6 = swap(after(at_6, x_5), "g")

    def sums(early_pieces, late_pieces):
        slot_0, slot_1 = (pick(early, e, l) for e, l in zip(early_pieces, late_pieces))
        return times_rows(grad_0, slot_0) + times_rows(grad_1, slot_1)

    due = sums((mine_0, mine_1), (at_2, at_3))
    there = swap(after(due, head_y), "b")
    due = sums((other_0, other_1), (x_2, x_3))
    first, due = lax.optimization_barrier((there, due))
    there = swap(due, "b")
    head_1, head_3 = swap(after(heads, x_2), "k"), swap(after(head_y, x_2), "k")
    kept_1 = sums((at_3, at_4), (mine_0, mine_1))
    due = sums((at_2, near_1), (at_5, at_4))
    second, due, kept_1, head_1, head_3 = lax.optimization_barrier((there, due, kept_1, head_1, head_3))
    there = swap(due, "b")

    head_all = [heads, head_1, head_y, head_3]

    def forward(rows, pieces, base=(), dtype=jnp.float32):
        numbers = [core]
        for row in rows:
            slot = 2 * (row // 2 != chip) + ((row & 1) != core)
            numbers += [slot, group, slot, 1 - group]
        return forward_sum(numbers, head_all, list(base), pieces, dtype)

    low = plane < 2
    near, far, far_next = plane ^ 1, pick(low, 2, 1), pick(low, 3, 0)
    rows_1 = [plane, near, pick(early, far, far_next), pick(early, far_next, far)]
    rows_0 = [plane, pick(early, near, far), pick(early, far, far_next), pick(early, far_next, near)]
    pieces_1 = [mine_1, other_1, near_1, x_1, at_4, x_4, pick(early, at_5, at_3), pick(early, x_5, x_3)]
    pieces_0 = [mine_0, other_0, at_2, x_2, pick(early, at_3, at_5), pick(early, x_3, x_5), at_6]
    total_1 = forward(rows_1, pieces_1)
    kept_2 = sums((x_3, x_4), (other_0, other_1))
    due = sums((x_2, x_1), (x_5, x_4))
    third, due, total_1, kept_2, x_6 = lax.optimization_barrier((there, due, total_1, kept_2, x_6))
    there = swap(due, "b")
    projected = forward(rows_0, pieces_0 + [x_6], [swap(total_1, "k")], jnp.bfloat16)

    kept_3 = sums((at_6, at_5), (at_6, near_1))
    kept_4 = sums((x_6, x_5), (x_6, x_1))
    done = [(k + t).astype(jnp.bfloat16) for k, t in ((kept_1, first), (kept_2, second), (kept_3, third))]
    done, kept_4, projected, there = lax.optimization_barrier((done, kept_4, projected, there))
    done.append((kept_4 + there).astype(jnp.bfloat16))
    first_mine = pick(early, plane // 2, plane & 1) == core
    head_grad = jnp.zeros_like(heads)
    for of_group, one, two in ((group, done[0], done[2]), (1 - group, done[1], done[3])):
        here = pick(first_mine, one, two)
        got = swap(pick(first_mine, two, one), "k")
        head_grad = lax.dynamic_update_slice_in_dim(head_grad, here, core * half + of_group * quarter, 1)
        head_grad = lax.dynamic_update_slice_in_dim(head_grad, got, (1 - core) * half + of_group * quarter, 1)
    return projected[None], head_grad[None]


def solution(mesh):
    n_group, n_row = mesh.shape["groups"], mesh.shape["row"]
    if (n_group, n_row) == (2, 16):
        grid = Mesh(mesh.devices.reshape(2, 4, 2, 2), ("g", "a", "b", "k"))
        tokens, whole = P(("a", "b", "k"), "g", None), P(("a", "b", "k"), None, None)
        body = grid_4
    else:
        grid = mesh
        tokens, whole = P("row", "groups", None), P("row", None, None)
        body = any_grid
    return jax.shard_map(
        body, mesh=grid, in_specs=(tokens, tokens, whole), out_specs=(tokens, tokens), check_vma=False
    )
```

```python
import functools

import jax
import jax.numpy as jnp
from jax import lax
from jax.experimental import pallas as pl
from jax.experimental.pallas import tpu as pltpu
from jax.sharding import Mesh
from jax.sharding import PartitionSpec as P


def partner_2(value, axis, distance):
    return lax.ppermute(value, axis, [(i, i ^ 1 << distance) for i in range(lax.axis_size(axis))])


def bit_at(device_index, position):
    return jnp.bitwise_and(jnp.right_shift(device_index, position), 1)


def grow_panel(own_block, bit_order, offset, device_index):
    panel = own_block
    for level_bit in bit_order:
        own_bit = bit_at(device_index, offset + level_bit)
        partner = partner_2(panel, "row", offset + level_bit)
        low_part = jnp.where(own_bit == 0, panel, partner)
        high_part = jnp.where(own_bit == 0, partner, panel)
        panel = jnp.stack([low_part, high_part], 0)
    return panel


def turn_panel(panel, layout, device_index, bit_order):
    for level_bit in bit_order:
        axis_at = layout.index(level_bit)
        own_bit = bit_at(device_index, level_bit)
        kept_half = lax.dynamic_index_in_dim(panel, own_bit, axis_at, keepdims=False)
        sent_half = lax.dynamic_index_in_dim(panel, 1 - own_bit, axis_at, keepdims=False)
        partner = partner_2(sent_half, "row", level_bit)
        low_part = jnp.where(own_bit == 0, kept_half, partner)
        high_part = jnp.where(own_bit == 0, partner, kept_half)
        panel = jnp.stack([low_part, high_part], axis_at)
    return panel


def any_grid(head_out, out_grad, proj_weight):
    levels = (lax.axis_size("row").bit_length() - 1) // 2
    device_index = lax.axis_index("row")
    bit_order = list(range(levels))
    layout = bit_order[::-1]
    letters = "pqrsuv"[:levels]
    head_panel = grow_panel(head_out[0], bit_order, 0, device_index)
    weight_panel = grow_panel(proj_weight[0], bit_order, levels, device_index)
    forward = jnp.einsum(
        letters + "ti," + letters + "io->to", head_panel, weight_panel, preferred_element_type=jnp.float32
    )
    turned = turn_panel(weight_panel, layout, device_index, bit_order)
    grad_panel = grow_panel(out_grad[0], bit_order, 0, device_index)
    summed = jnp.einsum(
        letters + "to," + letters + "io->ti", grad_panel, turned, preferred_element_type=jnp.float32
    )
    return forward.astype(jnp.bfloat16)[None], summed.astype(jnp.bfloat16)[None]


def swap(value, axis):
    return lax.ppermute(value, axis, [(0, 1), (1, 0)])


def send(value, pairs):
    return lax.ppermute(value, "a", pairs)


def after(value, *earlier):
    return lax.optimization_barrier((value, *earlier))[0]


def pick(flag, yes, no):
    return jnp.where(flag, yes, no)


def times(left, right):
    return lax.dot_general(left, right, (((1,), (0,)), ((), ())), preferred_element_type=jnp.float32)


def times_rows(left, right):
    return lax.dot_general(left, right, (((1,), (1,)), ((), ())), preferred_element_type=jnp.float32)


def sum_of_products(n_base, numbers, *refs):
    heads, base, pieces, out = refs[:4], refs[4 : 4 + n_base], refs[4 + n_base : -1], refs[-1]
    quarter = pieces[0].shape[0]
    total = None
    for term, piece in enumerate(pieces):
        slot, side = numbers[1 + 2 * term], numbers[2 + 2 * term]
        head = heads[3][...]
        for other in (2, 1, 0):
            head = jnp.where(slot == other, heads[other][...], head)
        head = jnp.where(side == 0, head[:, :quarter], head[:, quarter:])
        product = times(head, piece[...])
        total = product if total is None else total + product
    for term in base:
        total = total + term[...]
    out[...] = total.astype(out.dtype)


def kept_sums(flags, grad_0, grad_1, there, *refs):
    pieces, outs = refs[:8], refs[8:]
    flag = flags[0] != 0
    for number, out in enumerate(outs):
        early_0, early_1, late_0, late_1 = pieces[4 * number : 4 * number + 4]
        total = times_rows(grad_0[...], jnp.where(flag, early_0[...], late_0[...]))
        total = total + times_rows(grad_1[...], jnp.where(flag, early_1[...], late_1[...]))
        if number == 0:
            total = total + there[...]
        out[...] = total.astype(out.dtype)


def keep(early, grads, there, pieces):
    tokens, width = grads[0].shape
    quarter = pieces[0][0][0].shape[0]
    tile = tokens // 2
    by_rows = lambda columns: pl.BlockSpec((tile, columns), lambda i: (i, 0))
    flat = [p for four in pieces for two in four for p in two]
    return pl.pallas_call(
        kept_sums,
        grid=(tokens // tile,),
        in_specs=[pl.BlockSpec(memory_space=pltpu.SMEM)]
        + [by_rows(width)] * 2
        + [by_rows(quarter)]
        + [pl.BlockSpec(p.shape, lambda i: (0, 0), pipeline_mode=pl.Buffered(1)) for p in flat],
        out_specs=[by_rows(quarter)] * 2,
        out_shape=[jax.ShapeDtypeStruct((tokens, quarter), d) for d in (jnp.bfloat16, jnp.float32)],
        compiler_params=pltpu.CompilerParams(
            dimension_semantics=("arbitrary",), vmem_limit_bytes=60 * 1024 * 1024
        ),
        cost_estimate=pl.CostEstimate(flops=1000, bytes_accessed=1000, transcendentals=0),
    )(early.astype(jnp.int32).reshape(1), *grads, there, *flat)


def forward_sum(numbers, heads, base, pieces, dtype):
    tokens, width = heads[0].shape
    tile = tokens // 2
    by_rows = pl.BlockSpec((tile, width), lambda i, _: (i, 0))
    spec = pltpu.PrefetchScalarGridSpec(
        num_scalar_prefetch=1,
        grid=(tokens // tile,),
        in_specs=[pl.BlockSpec((tile, width // 2), lambda i, numbers: (i, numbers[0]))] * 4
        + [by_rows] * len(base)
        + [pl.BlockSpec(p.shape, lambda i, _: (0, 0), pipeline_mode=pl.Buffered(1)) for p in pieces],
        out_specs=by_rows,
    )
    return pl.pallas_call(
        functools.partial(sum_of_products, len(base)),
        grid_spec=spec,
        out_shape=jax.ShapeDtypeStruct((tokens, width), dtype),
        compiler_params=pltpu.CompilerParams(
            dimension_semantics=("arbitrary",), vmem_limit_bytes=60 * 1024 * 1024
        ),
        cost_estimate=pl.CostEstimate(flops=1000, bytes_accessed=1000, transcendentals=0),
    )(jnp.stack(numbers).astype(jnp.int32), *heads, *base, *pieces)


INWARD = [(0, 1), (3, 2)]
MIDDLE = [(1, 2), (2, 1)]
OUTWARD = [(1, 0), (2, 3)]
BOTH = INWARD + OUTWARD


def grid_4(head_out, out_grad, proj_weight):
    group = lax.axis_index("g")
    plane = lax.axis_index("a")
    chip = lax.axis_index("b")
    core = lax.axis_index("k")
    heads, grad_0, weight = head_out[0], out_grad[0], proj_weight[0]
    tokens, width = heads.shape
    half, quarter = width // 2, width // 4
    is_mid = (plane == 1) | (plane == 2)
    early = plane // 2 != chip

    def weight_rows(block, of_core, of_group):
        return lax.dynamic_slice_in_dim(block, of_core * half + of_group * quarter, quarter, 0)

    def sums(early_pieces, late_pieces):
        slot_0, slot_1 = (pick(early, e, l) for e, l in zip(early_pieces, late_pieces))
        return times_rows(grad_0, slot_0) + times_rows(grad_1, slot_1)

    mine_0 = weight_rows(weight, core, group)
    middle_0 = send(mine_0, MIDDLE)
    mine_1 = swap(weight_rows(after(weight, mine_0), 1 - core, group), "k")
    head_y = swap(heads, "b")
    near_1 = send(mine_1, BOTH)
    middle_1 = send(after(mine_1, near_1, middle_0), MIDDLE)
    grad_1 = swap(grad_0, "k")
    x_1 = swap(near_1, "g")
    ahead = is_mid & jnp.logical_not(early)
    mid_2 = pick(ahead, middle_0, mine_0)
    out_2 = send(after(mid_2, near_1), BOTH)
    cross_1 = send(after(near_1, middle_1), MIDDLE)
    mid_3 = pick(early, middle_0, after(middle_1, mid_2))
    out_3 = send(after(mid_3, out_2, x_1), OUTWARD)
    at_2 = pick(ahead, middle_0, after(out_2, mid_3))
    x_2 = swap(after(at_2, x_1, grad_1), "g")
    cross_0 = send(after(out_2, cross_1), MIDDLE)
    late_weight = after(weight, x_1)
    other_0 = weight_rows(late_weight, core, 1 - group)
    other_1 = swap(weight_rows(late_weight, 1 - core, 1 - group), "k")
    mid_4 = pick(early, middle_1, after(cross_1, at_2))
    out_4 = send(after(mid_4, out_3), OUTWARD)
    at_3 = pick(is_mid, mid_3, after(out_3, x_1, other_0, other_1, mid_4, head_y))
    due_1 = sums((mine_0, mine_1), (at_2, at_3))
    x_3 = swap(after(at_3, x_2, due_1), "g")

    there = swap(after(due_1, head_y), "b")
    due = sums((other_0, other_1), (x_2, x_3))
    first, due = lax.optimization_barrier((there, due))
    there = swap(due, "b")
    mid_5 = pick(early, cross_1, after(cross_0, at_3))
    out_5 = send(after(mid_5, out_4), OUTWARD)
    at_4 = pick(is_mid, mid_4, after(out_4, x_2, mid_5))
    x_4 = swap(after(at_4, x_3), "g")
    late_6 = pick(early, cross_0, after(mine_0, at_4))
    out_6 = send(after(late_6, out_5), OUTWARD)
    at_5 = pick(is_mid, mid_5, after(out_5, x_3, late_6))
    x_5 = swap(after(at_5, x_4), "g")

    head_1, head_3 = swap(after(heads, x_2), "k"), swap(after(head_y, x_2), "k")
    due = sums((at_2, near_1), (at_5, at_4))
    kept_1 = sums(*after(((at_3, at_4), (mine_0, mine_1)), first))
    kept_2 = sums((x_3, x_4), (other_0, other_1))
    second, due, head_1, head_3, kept_1, kept_2 = lax.optimization_barrier(
        (there, due, head_1, head_3, kept_1, kept_2)
    )
    there = swap(due, "b")
    at_6 = pick(is_mid, pick(early, cross_0, out_2), after(out_6, second))
    x_6 = swap(after(at_6, x_5), "g")

    head_all = [heads, head_1, head_y, head_3]

    def forward(rows, pieces, base=(), dtype=jnp.float32):
        numbers = [core]
        for row in rows:
            slot = 2 * (row // 2 != chip) + ((row & 1) != core)
            numbers += [slot, group, slot, 1 - group]
        return forward_sum(numbers, head_all, list(base), pieces, dtype)

    low = plane < 2
    near, far, far_next = plane ^ 1, pick(low, 2, 1), pick(low, 3, 0)
    rows_1 = [plane, near, pick(early, far, far_next), pick(early, far_next, far)]
    rows_0 = [plane, pick(early, near, far), pick(early, far, far_next), pick(early, far_next, near)]
    pieces_1 = [mine_1, other_1, near_1, x_1, at_4, x_4, pick(early, at_5, at_3), pick(early, x_5, x_3)]
    pieces_0 = [mine_0, other_0, at_2, x_2, pick(early, at_3, at_5), pick(early, x_3, x_5), at_6]
    total_1 = forward(rows_1, pieces_1)
    due = sums((x_2, x_1), (x_5, x_4))
    third, due, total_1, x_6 = lax.optimization_barrier((there, due, total_1, x_6))
    there = swap(due, "b")
    other_part = swap(total_1, "k")
    projected = forward(rows_0, pieces_0 + [x_6], [other_part], jnp.bfloat16)

    done = [(k + t).astype(jnp.bfloat16) for k, t in ((kept_1, first), (kept_2, second))]
    last, kept = keep(
        early, [grad_0, grad_1], third, [((at_6, at_5), (at_6, near_1)), ((x_6, x_5), (x_6, x_1))]
    )
    done.append(last)
    first_mine = pick(early, plane // 2, plane & 1) == core
    here_z, got_z = pick(first_mine, done[0], done[2]), swap(pick(first_mine, done[2], done[0]), "k")
    done, kept, projected, here_z, got_z, there = lax.optimization_barrier(
        (done, kept, projected, here_z, got_z, there)
    )
    done.append((kept + there).astype(jnp.bfloat16))
    here_x, got_x = pick(first_mine, done[1], done[3]), swap(pick(first_mine, done[3], done[1]), "k")
    head_grad = jnp.zeros_like(heads)
    for of_core, of_group, part in (
        (core, group, here_z),
        (1 - core, group, got_z),
        (core, 1 - group, here_x),
        (1 - core, 1 - group, got_x),
    ):
        head_grad = lax.dynamic_update_slice_in_dim(head_grad, part, of_core * half + of_group * quarter, 1)
    return projected[None], head_grad[None]


def solution(mesh):
    n_group, n_row = mesh.shape["groups"], mesh.shape["row"]
    if (n_group, n_row) == (2, 16):
        grid = Mesh(mesh.devices.reshape(2, 4, 2, 2), ("g", "a", "b", "k"))
        tokens, whole = P(("a", "b", "k"), "g", None), P(("a", "b", "k"), None, None)
        body = grid_4
    else:
        grid = mesh
        tokens, whole = P("row", "groups", None), P("row", None, None)
        body = any_grid
    return jax.shard_map(
        body, mesh=grid, in_specs=(tokens, tokens, whole), out_specs=(tokens, tokens), check_vma=False
    )
```

```python
import functools

import jax
import jax.numpy as jnp
from jax import lax
from jax.experimental import pallas as pl
from jax.experimental.pallas import tpu as pltpu
from jax.sharding import Mesh
from jax.sharding import PartitionSpec as P


def partner_2(value, axis, distance):
    return lax.ppermute(value, axis, [(i, i ^ 1 << distance) for i in range(lax.axis_size(axis))])


def bit_at(device_index, position):
    return jnp.bitwise_and(jnp.right_shift(device_index, position), 1)


def grow_panel(own_block, bit_order, offset, device_index):
    panel = own_block
    for level_bit in bit_order:
        own_bit = bit_at(device_index, offset + level_bit)
        partner = partner_2(panel, "row", offset + level_bit)
        low_part = jnp.where(own_bit == 0, panel, partner)
        high_part = jnp.where(own_bit == 0, partner, panel)
        panel = jnp.stack([low_part, high_part], 0)
    return panel


def turn_panel(panel, layout, device_index, bit_order):
    for level_bit in bit_order:
        axis_at = layout.index(level_bit)
        own_bit = bit_at(device_index, level_bit)
        kept_half = lax.dynamic_index_in_dim(panel, own_bit, axis_at, keepdims=False)
        sent_half = lax.dynamic_index_in_dim(panel, 1 - own_bit, axis_at, keepdims=False)
        partner = partner_2(sent_half, "row", level_bit)
        low_part = jnp.where(own_bit == 0, kept_half, partner)
        high_part = jnp.where(own_bit == 0, partner, kept_half)
        panel = jnp.stack([low_part, high_part], axis_at)
    return panel


def any_grid(head_out, out_grad, proj_weight):
    levels = (lax.axis_size("row").bit_length() - 1) // 2
    device_index = lax.axis_index("row")
    bit_order = list(range(levels))
    layout = bit_order[::-1]
    letters = "pqrsuv"[:levels]
    head_panel = grow_panel(head_out[0], bit_order, 0, device_index)
    weight_panel = grow_panel(proj_weight[0], bit_order, levels, device_index)
    forward = jnp.einsum(
        letters + "ti," + letters + "io->to", head_panel, weight_panel, preferred_element_type=jnp.float32
    )
    turned = turn_panel(weight_panel, layout, device_index, bit_order)
    grad_panel = grow_panel(out_grad[0], bit_order, 0, device_index)
    summed = jnp.einsum(
        letters + "to," + letters + "io->ti", grad_panel, turned, preferred_element_type=jnp.float32
    )
    return forward.astype(jnp.bfloat16)[None], summed.astype(jnp.bfloat16)[None]


def swap(value, axis):
    return lax.ppermute(value, axis, [(0, 1), (1, 0)])


def send(value, pairs):
    return lax.ppermute(value, "a", pairs)


def after(value, *earlier):
    return lax.optimization_barrier((value, *earlier))[0]


def pick(flag, yes, no):
    return jnp.where(flag, yes, no)


def times(left, right):
    return lax.dot_general(left, right, (((1,), (0,)), ((), ())), preferred_element_type=jnp.float32)


def times_rows(left, right):
    return lax.dot_general(left, right, (((1,), (1,)), ((), ())), preferred_element_type=jnp.float32)


def sum_of_products(n_base, numbers, *refs):
    heads, base, pieces, out = refs[:4], refs[4 : 4 + n_base], refs[4 + n_base : -1], refs[-1]
    quarter = pieces[0].shape[0]
    total = None
    for term, piece in enumerate(pieces):
        slot, side = numbers[1 + 2 * term], numbers[2 + 2 * term]
        head = heads[3][...]
        for other in (2, 1, 0):
            head = jnp.where(slot == other, heads[other][...], head)
        head = jnp.where(side == 0, head[:, :quarter], head[:, quarter:])
        product = times(head, piece[...])
        total = product if total is None else total + product
    for term in base:
        total = total + term[...]
    out[...] = total.astype(out.dtype)


def kept_sums(flags, grad_0, grad_1, there, *refs):
    pieces, outs = refs[:8], refs[8:]
    flag = flags[0] != 0
    for number, out in enumerate(outs):
        early_0, early_1, late_0, late_1 = pieces[4 * number : 4 * number + 4]
        total = times_rows(grad_0[...], jnp.where(flag, early_0[...], late_0[...]))
        total = total + times_rows(grad_1[...], jnp.where(flag, early_1[...], late_1[...]))
        if number == 0:
            total = total + there[...]
        out[...] = total.astype(out.dtype)


def keep(early, grads, there, pieces):
    tokens, width = grads[0].shape
    quarter = pieces[0][0][0].shape[0]
    tile = tokens // 2
    by_rows = lambda columns: pl.BlockSpec((tile, columns), lambda i: (i, 0))
    flat = [p for four in pieces for two in four for p in two]
    return pl.pallas_call(
        kept_sums,
        grid=(tokens // tile,),
        in_specs=[pl.BlockSpec(memory_space=pltpu.SMEM)]
        + [by_rows(width)] * 2
        + [by_rows(quarter)]
        + [pl.BlockSpec(p.shape, lambda i: (0, 0), pipeline_mode=pl.Buffered(1)) for p in flat],
        out_specs=[by_rows(quarter)] * 2,
        out_shape=[jax.ShapeDtypeStruct((tokens, quarter), d) for d in (jnp.bfloat16, jnp.float32)],
        compiler_params=pltpu.CompilerParams(
            dimension_semantics=("arbitrary",), vmem_limit_bytes=60 * 1024 * 1024
        ),
        cost_estimate=pl.CostEstimate(flops=1000, bytes_accessed=1000, transcendentals=0),
    )(early.astype(jnp.int32).reshape(1), *grads, there, *flat)


def forward_sum(numbers, heads, base, pieces, dtype):
    tokens, width = heads[0].shape
    tile = tokens // 2
    by_rows = pl.BlockSpec((tile, width), lambda i, _: (i, 0))
    spec = pltpu.PrefetchScalarGridSpec(
        num_scalar_prefetch=1,
        grid=(tokens // tile,),
        in_specs=[pl.BlockSpec((tile, width // 2), lambda i, numbers: (i, numbers[0]))] * 4
        + [by_rows] * len(base)
        + [pl.BlockSpec(p.shape, lambda i, _: (0, 0), pipeline_mode=pl.Buffered(1)) for p in pieces],
        out_specs=by_rows,
    )
    return pl.pallas_call(
        functools.partial(sum_of_products, len(base)),
        grid_spec=spec,
        out_shape=jax.ShapeDtypeStruct((tokens, width), dtype),
        compiler_params=pltpu.CompilerParams(
            dimension_semantics=("arbitrary",), vmem_limit_bytes=60 * 1024 * 1024
        ),
        cost_estimate=pl.CostEstimate(flops=1000, bytes_accessed=1000, transcendentals=0),
    )(numbers, *heads, *base, *pieces)


INWARD = [(0, 1), (3, 2)]
MIDDLE = [(1, 2), (2, 1)]
OUTWARD = [(1, 0), (2, 3)]
BOTH = INWARD + OUTWARD


def grid_4(head_out, out_grad, proj_weight):
    group = lax.axis_index("g")
    plane = lax.axis_index("a")
    chip = lax.axis_index("b")
    core = lax.axis_index("k")
    heads, grad_0, weight = head_out[0], out_grad[0], proj_weight[0]
    tokens, width = heads.shape
    half, quarter = width // 2, width // 4
    is_mid = (plane == 1) | (plane == 2)
    early = plane // 2 != chip

    def weight_rows(block, of_core, of_group):
        return lax.dynamic_slice_in_dim(block, of_core * half + of_group * quarter, quarter, 0)

    def sums(early_pieces, late_pieces):
        slot_0, slot_1 = (pick(early, e, l) for e, l in zip(early_pieces, late_pieces))
        return times_rows(grad_0, slot_0) + times_rows(grad_1, slot_1)

    low = plane < 2
    near, far, far_next = plane ^ 1, pick(low, 2, 1), pick(low, 3, 0)

    def numbers_of(rows):
        numbers = [core]
        for row in rows:
            slot = 2 * (row // 2 != chip) + ((row & 1) != core)
            numbers += [slot, group, slot, 1 - group]
        return jnp.stack(numbers).astype(jnp.int32)

    numbers_1 = numbers_of([plane, near, pick(early, far, far_next), pick(early, far_next, far)])
    numbers_0 = numbers_of([plane, pick(early, near, far), pick(early, far, far_next), pick(early, far_next, near)])

    mine_0 = weight_rows(weight, core, group)
    middle_0 = send(mine_0, MIDDLE)
    mine_1 = swap(weight_rows(after(weight, mine_0), 1 - core, group), "k")
    head_y = swap(heads, "b")
    near_1 = send(mine_1, BOTH)
    middle_1 = send(after(mine_1, near_1, middle_0), MIDDLE)
    grad_1 = swap(grad_0, "k")
    x_1 = swap(near_1, "g")
    ahead = is_mid & jnp.logical_not(early)
    mid_2 = pick(ahead, middle_0, mine_0)
    out_2 = send(after(mid_2, near_1), BOTH)
    cross_1 = send(after(near_1, middle_1), MIDDLE)
    mid_3 = pick(early, middle_0, after(middle_1, mid_2))
    out_3 = send(after(mid_3, out_2, x_1), OUTWARD)
    at_2 = pick(ahead, middle_0, after(out_2, mid_3))
    x_2 = swap(after(at_2, x_1, grad_1), "g")
    cross_0 = send(after(out_2, cross_1), MIDDLE)
    late_weight = after(weight, x_1)
    other_0 = weight_rows(late_weight, core, 1 - group)
    other_1 = swap(weight_rows(late_weight, 1 - core, 1 - group), "k")
    mid_4 = pick(early, middle_1, after(cross_1, at_2))
    out_4 = send(after(mid_4, out_3), OUTWARD)
    at_3 = pick(is_mid, mid_3, after(out_3, x_1, other_0, other_1, mid_4, head_y))
    due_1 = sums((mine_0, mine_1), (at_2, at_3))
    x_3 = swap(after(at_3, x_2, due_1), "g")

    there = swap(after(due_1, head_y), "b")
    due = sums((other_0, other_1), (x_2, x_3))
    first, due, numbers_0, numbers_1 = lax.optimization_barrier((there, due, numbers_0, numbers_1))
    there = swap(due, "b")
    mid_5 = pick(early, cross_1, after(cross_0, at_3))
    out_5 = send(after(mid_5, out_4), OUTWARD)
    at_4 = pick(is_mid, mid_4, after(out_4, x_2, mid_5))
    x_4 = swap(after(at_4, x_3), "g")
    late_6 = pick(early, cross_0, after(mine_0, at_4))
    out_6 = send(after(late_6, out_5), OUTWARD)
    at_5 = pick(is_mid, mid_5, after(out_5, x_3, late_6))
    x_5 = swap(after(at_5, x_4), "g")

    head_1, head_3 = swap(after(heads, x_2), "k"), swap(after(head_y, x_2), "k")
    due = sums((at_2, near_1), (at_5, at_4))
    kept_1 = sums(*after(((at_3, at_4), (mine_0, mine_1)), first))
    kept_2 = sums((x_3, x_4), (other_0, other_1))
    second, due, head_1, head_3, kept_1, kept_2 = lax.optimization_barrier(
        (there, due, head_1, head_3, kept_1, kept_2)
    )
    there = swap(due, "b")
    at_6 = pick(is_mid, pick(early, cross_0, out_2), after(out_6, second))
    x_6 = swap(after(at_6, x_5), "g")

    head_all = [heads, head_1, head_y, head_3]

    pieces_1 = [mine_1, other_1, near_1, x_1, at_4, x_4, pick(early, at_5, at_3), pick(early, x_5, x_3)]
    pieces_0 = [mine_0, other_0, at_2, x_2, pick(early, at_3, at_5), pick(early, x_3, x_5), at_6]
    total_1 = forward_sum(numbers_1, head_all, [], pieces_1, jnp.float32)
    due = sums((x_2, x_1), (x_5, x_4))
    third, due, total_1, x_6 = lax.optimization_barrier((there, due, total_1, x_6))
    there = swap(due, "b")
    other_part = swap(total_1, "k")
    projected = forward_sum(numbers_0, head_all, [other_part], pieces_0 + [x_6], jnp.bfloat16)

    done = [(k + t).astype(jnp.bfloat16) for k, t in ((kept_1, first), (kept_2, second))]
    last, kept = keep(
        early, [grad_0, grad_1], third, [((at_6, at_5), (at_6, near_1)), ((x_6, x_5), (x_6, x_1))]
    )
    done.append(last)
    first_mine = pick(early, plane // 2, plane & 1) == core
    here_z, got_z = pick(first_mine, done[0], done[2]), swap(pick(first_mine, done[2], done[0]), "k")
    done, kept, projected, here_z, got_z, there = lax.optimization_barrier(
        (done, kept, projected, here_z, got_z, there)
    )
    done.append((kept + there).astype(jnp.bfloat16))
    here_x, got_x = pick(first_mine, done[1], done[3]), swap(pick(first_mine, done[3], done[1]), "k")
    head_grad = jnp.zeros_like(heads)
    for of_core, of_group, part in (
        (core, group, here_z),
        (1 - core, group, got_z),
        (core, 1 - group, here_x),
        (1 - core, 1 - group, got_x),
    ):
        head_grad = lax.dynamic_update_slice_in_dim(head_grad, part, of_core * half + of_group * quarter, 1)
    return projected[None], head_grad[None]


def solution(mesh):
    n_group, n_row = mesh.shape["groups"], mesh.shape["row"]
    if (n_group, n_row) == (2, 16):
        grid = Mesh(mesh.devices.reshape(2, 4, 2, 2), ("g", "a", "b", "k"))
        tokens, whole = P(("a", "b", "k"), "g", None), P(("a", "b", "k"), None, None)
        body = grid_4
    else:
        grid = mesh
        tokens, whole = P("row", "groups", None), P("row", None, None)
        body = any_grid
    return jax.shard_map(
        body, mesh=grid, in_specs=(tokens, tokens, whole), out_specs=(tokens, tokens), check_vma=False
    )
```

```python
import functools

import jax
import jax.numpy as jnp
from jax import lax
from jax.experimental import pallas as pl
from jax.experimental.pallas import tpu as pltpu
from jax.sharding import Mesh
from jax.sharding import PartitionSpec as P


def partner_2(value, axis, distance):
    return lax.ppermute(value, axis, [(i, i ^ 1 << distance) for i in range(lax.axis_size(axis))])


def bit_at(device_index, position):
    return jnp.bitwise_and(jnp.right_shift(device_index, position), 1)


def grow_panel(own_block, bit_order, offset, device_index):
    panel = own_block
    for level_bit in bit_order:
        own_bit = bit_at(device_index, offset + level_bit)
        partner = partner_2(panel, "row", offset + level_bit)
        low_part = jnp.where(own_bit == 0, panel, partner)
        high_part = jnp.where(own_bit == 0, partner, panel)
        panel = jnp.stack([low_part, high_part], 0)
    return panel


def turn_panel(panel, layout, device_index, bit_order):
    for level_bit in bit_order:
        axis_at = layout.index(level_bit)
        own_bit = bit_at(device_index, level_bit)
        kept_half = lax.dynamic_index_in_dim(panel, own_bit, axis_at, keepdims=False)
        sent_half = lax.dynamic_index_in_dim(panel, 1 - own_bit, axis_at, keepdims=False)
        partner = partner_2(sent_half, "row", level_bit)
        low_part = jnp.where(own_bit == 0, kept_half, partner)
        high_part = jnp.where(own_bit == 0, partner, kept_half)
        panel = jnp.stack([low_part, high_part], axis_at)
    return panel


def any_grid(head_out, out_grad, proj_weight):
    levels = (lax.axis_size("row").bit_length() - 1) // 2
    device_index = lax.axis_index("row")
    bit_order = list(range(levels))
    layout = bit_order[::-1]
    letters = "pqrsuv"[:levels]
    head_panel = grow_panel(head_out[0], bit_order, 0, device_index)
    weight_panel = grow_panel(proj_weight[0], bit_order, levels, device_index)
    forward = jnp.einsum(
        letters + "ti," + letters + "io->to", head_panel, weight_panel, preferred_element_type=jnp.float32
    )
    turned = turn_panel(weight_panel, layout, device_index, bit_order)
    grad_panel = grow_panel(out_grad[0], bit_order, 0, device_index)
    summed = jnp.einsum(
        letters + "to," + letters + "io->ti", grad_panel, turned, preferred_element_type=jnp.float32
    )
    return forward.astype(jnp.bfloat16)[None], summed.astype(jnp.bfloat16)[None]


def swap(value, axis):
    return lax.ppermute(value, axis, [(0, 1), (1, 0)])


def send(value, pairs):
    return lax.ppermute(value, "a", pairs)


def after(value, *earlier):
    return lax.optimization_barrier((value, *earlier))[0]


def pick(flag, yes, no):
    return jnp.where(flag, yes, no)


def times(left, right):
    return lax.dot_general(left, right, (((1,), (0,)), ((), ())), preferred_element_type=jnp.float32)


def times_rows(left, right):
    return lax.dot_general(left, right, (((1,), (1,)), ((), ())), preferred_element_type=jnp.float32)


def sum_of_products(n_base, numbers, *refs):
    heads, base, pieces, out = refs[:4], refs[4 : 4 + n_base], refs[4 + n_base : -1], refs[-1]
    quarter = pieces[0].shape[0]
    total = None
    for term, piece in enumerate(pieces):
        slot, side = numbers[1 + 2 * term], numbers[2 + 2 * term]
        head = heads[3][...]
        for other in (2, 1, 0):
            head = jnp.where(slot == other, heads[other][...], head)
        head = jnp.where(side == 0, head[:, :quarter], head[:, quarter:])
        product = times(head, piece[...])
        total = product if total is None else total + product
    for term in base:
        total = total + term[...]
    out[...] = total.astype(out.dtype)


def kept_sums(flags, grad_0, grad_1, there, *refs):
    pieces, outs = refs[:8], refs[8:]
    flag = flags[0] != 0
    for number, out in enumerate(outs):
        early_0, early_1, late_0, late_1 = pieces[4 * number : 4 * number + 4]
        total = times_rows(grad_0[...], jnp.where(flag, early_0[...], late_0[...]))
        total = total + times_rows(grad_1[...], jnp.where(flag, early_1[...], late_1[...]))
        if number == 0:
            total = total + there[...]
        out[...] = total.astype(out.dtype)


def keep(early, grads, there, pieces):
    tokens, width = grads[0].shape
    quarter = pieces[0][0][0].shape[0]
    tile = tokens // 2
    by_rows = lambda columns: pl.BlockSpec((tile, columns), lambda i: (i, 0))
    flat = [p for four in pieces for two in four for p in two]
    return pl.pallas_call(
        kept_sums,
        grid=(tokens // tile,),
        in_specs=[pl.BlockSpec(memory_space=pltpu.SMEM)]
        + [by_rows(width)] * 2
        + [by_rows(quarter)]
        + [pl.BlockSpec(p.shape, lambda i: (0, 0), pipeline_mode=pl.Buffered(1)) for p in flat],
        out_specs=[by_rows(quarter)] * 2,
        out_shape=[jax.ShapeDtypeStruct((tokens, quarter), d) for d in (jnp.bfloat16, jnp.float32)],
        compiler_params=pltpu.CompilerParams(
            dimension_semantics=("arbitrary",), vmem_limit_bytes=60 * 1024 * 1024
        ),
        cost_estimate=pl.CostEstimate(flops=1000, bytes_accessed=1000, transcendentals=0),
    )(early.astype(jnp.int32).reshape(1), *grads, there, *flat)


def forward_sum(numbers, heads, base, pieces, dtype):
    tokens, width = heads[0].shape
    tile = tokens // 2
    by_rows = pl.BlockSpec((tile, width), lambda i, _: (i, 0))
    spec = pltpu.PrefetchScalarGridSpec(
        num_scalar_prefetch=1,
        grid=(tokens // tile,),
        in_specs=[pl.BlockSpec((tile, width // 2), lambda i, numbers: (i, numbers[0]))] * 4
        + [by_rows] * len(base)
        + [pl.BlockSpec(p.shape, lambda i, _: (0, 0), pipeline_mode=pl.Buffered(1)) for p in pieces],
        out_specs=by_rows,
    )
    return pl.pallas_call(
        functools.partial(sum_of_products, len(base)),
        grid_spec=spec,
        out_shape=jax.ShapeDtypeStruct((tokens, width), dtype),
        compiler_params=pltpu.CompilerParams(
            dimension_semantics=("arbitrary",), vmem_limit_bytes=60 * 1024 * 1024
        ),
        cost_estimate=pl.CostEstimate(flops=1000, bytes_accessed=1000, transcendentals=0),
    )(numbers, *heads, *base, *pieces)


INWARD = [(0, 1), (3, 2)]
MIDDLE = [(1, 2), (2, 1)]
OUTWARD = [(1, 0), (2, 3)]
BOTH = INWARD + OUTWARD


def grid_4(head_out, out_grad, proj_weight):
    group = lax.axis_index("g")
    plane = lax.axis_index("a")
    chip = lax.axis_index("b")
    core = lax.axis_index("k")
    heads, grad_0, weight = head_out[0], out_grad[0], proj_weight[0]
    tokens, width = heads.shape
    half, quarter = width // 2, width // 4
    is_mid = (plane == 1) | (plane == 2)
    early = plane // 2 != chip

    def weight_rows(block, of_core, of_group):
        return lax.dynamic_slice_in_dim(block, of_core * half + of_group * quarter, quarter, 0)

    def sums(early_pieces, late_pieces):
        slot_0, slot_1 = (pick(early, e, l) for e, l in zip(early_pieces, late_pieces))
        return times_rows(grad_0, slot_0) + times_rows(grad_1, slot_1)

    low = plane < 2
    near, far, far_next = plane ^ 1, pick(low, 2, 1), pick(low, 3, 0)

    def numbers_of(rows):
        numbers = [core]
        for row in rows:
            slot = 2 * (row // 2 != chip) + ((row & 1) != core)
            numbers += [slot, group, slot, 1 - group]
        return jnp.stack(numbers).astype(jnp.int32)

    numbers_1 = numbers_of([plane, near, pick(early, far, far_next), pick(early, far_next, far)])
    numbers_0 = numbers_of([plane, pick(early, near, far), pick(early, far, far_next), pick(early, far_next, near)])

    mine_0 = weight_rows(weight, core, group)
    middle_0 = send(mine_0, MIDDLE)
    mine_1 = swap(weight_rows(after(weight, mine_0), 1 - core, group), "k")
    head_y = swap(heads, "b")
    near_1 = send(mine_1, BOTH)
    middle_1 = send(after(mine_1, near_1, middle_0), MIDDLE)
    grad_1 = swap(grad_0, "k")
    x_1 = swap(near_1, "g")
    ahead = is_mid & jnp.logical_not(early)
    mid_2 = pick(ahead, middle_0, mine_0)
    out_2 = send(after(mid_2, near_1), BOTH)
    cross_1 = send(after(near_1, middle_1), MIDDLE)
    mid_3 = pick(early, middle_0, after(middle_1, mid_2))
    out_3 = send(after(mid_3, out_2, x_1), OUTWARD)
    at_2 = pick(ahead, middle_0, after(out_2, mid_3))
    x_2 = swap(after(at_2, x_1, grad_1), "g")
    cross_0 = send(after(out_2, cross_1), MIDDLE)
    late_weight = after(weight, x_1)
    other_0 = weight_rows(late_weight, core, 1 - group)
    other_1 = swap(weight_rows(late_weight, 1 - core, 1 - group), "k")
    mid_4 = pick(early, middle_1, after(cross_1, at_2))
    out_4 = send(after(mid_4, out_3), OUTWARD)
    at_3 = pick(is_mid, mid_3, after(out_3, x_1, other_0, other_1, mid_4, head_y))
    due_1 = sums((mine_0, mine_1), (at_2, at_3))
    x_3 = swap(after(at_3, x_2, due_1), "g")

    there = swap(after(due_1, head_y), "b")
    due = sums((other_0, other_1), (x_2, x_3))
    first, due, numbers_0, numbers_1 = lax.optimization_barrier((there, due, numbers_0, numbers_1))
    there = swap(due, "b")
    mid_5 = pick(early, cross_1, after(cross_0, at_3))
    out_5 = send(after(mid_5, out_4), OUTWARD)
    at_4 = pick(is_mid, mid_4, after(out_4, x_2, mid_5))
    x_4 = swap(after(at_4, x_3), "g")
    late_6 = pick(early, cross_0, after(mine_0, at_4))
    out_6 = send(after(late_6, out_5), OUTWARD)
    at_5 = pick(is_mid, mid_5, after(out_5, x_3, late_6))
    x_5 = swap(after(at_5, x_4), "g")

    head_1, head_3 = swap(after(heads, x_2), "k"), swap(after(head_y, x_2), "k")
    due = sums((at_2, near_1), (at_5, at_4))
    kept_1 = sums(*after(((at_3, at_4), (mine_0, mine_1)), first))
    kept_2 = sums((x_3, x_4), (other_0, other_1))
    second, due, head_1, head_3, kept_1, kept_2 = lax.optimization_barrier(
        (there, due, head_1, head_3, kept_1, kept_2)
    )
    there = swap(due, "b")
    at_6 = pick(is_mid, pick(early, cross_0, out_2), after(out_6, second))
    x_6 = swap(after(at_6, x_5), "g")

    head_all = [heads, head_1, head_y, head_3]

    pieces_1 = [mine_1, other_1, near_1, x_1, at_4, x_4, pick(early, at_5, at_3), pick(early, x_5, x_3)]
    pieces_0 = [mine_0, other_0, at_2, x_2, pick(early, at_3, at_5), pick(early, x_3, x_5), at_6]
    total_1 = forward_sum(numbers_1, head_all, [], pieces_1, jnp.float32)
    due = sums((x_2, x_1), (x_5, x_4))
    third, due, total_1, x_6 = lax.optimization_barrier((there, due, total_1, x_6))
    there = swap(due, "b")
    other_part = swap(total_1, "k")
    projected = forward_sum(numbers_0, head_all, [other_part], pieces_0 + [x_6], jnp.bfloat16)

    done = [(k + t).astype(jnp.bfloat16) for k, t in ((kept_1, first), (kept_2, second))]
    last, kept = keep(
        early, [grad_0, grad_1], third, [((at_6, at_5), (at_6, near_1)), ((x_6, x_5), (x_6, x_1))]
    )
    done.append(last)
    first_mine = pick(early, plane // 2, plane & 1) == core
    here_z, got_z = pick(first_mine, done[0], done[2]), swap(pick(first_mine, done[2], done[0]), "k")
    head_grad = jnp.zeros_like(heads)
    for of_core, part in ((core, here_z), (1 - core, got_z)):
        head_grad = lax.dynamic_update_slice_in_dim(head_grad, part, of_core * half + group * quarter, 1)
    done, kept, projected, head_grad, there = lax.optimization_barrier((done, kept, projected, head_grad, there))
    done.append((kept + there).astype(jnp.bfloat16))
    here_x, got_x = pick(first_mine, done[1], done[3]), swap(pick(first_mine, done[3], done[1]), "k")
    for of_core, part in ((core, here_x), (1 - core, got_x)):
        head_grad = lax.dynamic_update_slice_in_dim(head_grad, part, of_core * half + (1 - group) * quarter, 1)
    return projected[None], head_grad[None]


def solution(mesh):
    n_group, n_row = mesh.shape["groups"], mesh.shape["row"]
    if (n_group, n_row) == (2, 16):
        grid = Mesh(mesh.devices.reshape(2, 4, 2, 2), ("g", "a", "b", "k"))
        tokens, whole = P(("a", "b", "k"), "g", None), P(("a", "b", "k"), None, None)
        body = grid_4
    else:
        grid = mesh
        tokens, whole = P("row", "groups", None), P("row", None, None)
        body = any_grid
    return jax.shard_map(
        body, mesh=grid, in_specs=(tokens, tokens, whole), out_specs=(tokens, tokens), check_vma=False
    )
```

```python
import functools

import jax
import jax.numpy as jnp
from jax import lax
from jax.experimental import pallas as pl
from jax.experimental.pallas import tpu as pltpu
from jax.sharding import Mesh
from jax.sharding import PartitionSpec as P


def partner_2(value, axis, distance):
    return lax.ppermute(value, axis, [(i, i ^ 1 << distance) for i in range(lax.axis_size(axis))])


def bit_at(device_index, position):
    return jnp.bitwise_and(jnp.right_shift(device_index, position), 1)


def grow_panel(own_block, bit_order, offset, device_index):
    panel = own_block
    for level_bit in bit_order:
        own_bit = bit_at(device_index, offset + level_bit)
        partner = partner_2(panel, "row", offset + level_bit)
        low_part = jnp.where(own_bit == 0, panel, partner)
        high_part = jnp.where(own_bit == 0, partner, panel)
        panel = jnp.stack([low_part, high_part], 0)
    return panel


def turn_panel(panel, layout, device_index, bit_order):
    for level_bit in bit_order:
        axis_at = layout.index(level_bit)
        own_bit = bit_at(device_index, level_bit)
        kept_half = lax.dynamic_index_in_dim(panel, own_bit, axis_at, keepdims=False)
        sent_half = lax.dynamic_index_in_dim(panel, 1 - own_bit, axis_at, keepdims=False)
        partner = partner_2(sent_half, "row", level_bit)
        low_part = jnp.where(own_bit == 0, kept_half, partner)
        high_part = jnp.where(own_bit == 0, partner, kept_half)
        panel = jnp.stack([low_part, high_part], axis_at)
    return panel


def any_grid(head_out, out_grad, proj_weight):
    levels = (lax.axis_size("row").bit_length() - 1) // 2
    device_index = lax.axis_index("row")
    bit_order = list(range(levels))
    layout = bit_order[::-1]
    letters = "pqrsuv"[:levels]
    head_panel = grow_panel(head_out[0], bit_order, 0, device_index)
    weight_panel = grow_panel(proj_weight[0], bit_order, levels, device_index)
    forward = jnp.einsum(
        letters + "ti," + letters + "io->to", head_panel, weight_panel, preferred_element_type=jnp.float32
    )
    turned = turn_panel(weight_panel, layout, device_index, bit_order)
    grad_panel = grow_panel(out_grad[0], bit_order, 0, device_index)
    summed = jnp.einsum(
        letters + "to," + letters + "io->ti", grad_panel, turned, preferred_element_type=jnp.float32
    )
    return forward.astype(jnp.bfloat16)[None], summed.astype(jnp.bfloat16)[None]


def swap(value, axis):
    return lax.ppermute(value, axis, [(0, 1), (1, 0)])


def send(value, pairs):
    return lax.ppermute(value, "a", pairs)


def after(value, *earlier):
    return lax.optimization_barrier((value, *earlier))[0]


def pick(flag, yes, no):
    return jnp.where(flag, yes, no)


def times(left, right):
    return lax.dot_general(left, right, (((1,), (0,)), ((), ())), preferred_element_type=jnp.float32)


def times_rows(left, right):
    return lax.dot_general(left, right, (((1,), (1,)), ((), ())), preferred_element_type=jnp.float32)


def sum_of_products(n_base, numbers, *refs):
    heads, base, pieces, out = refs[:4], refs[4 : 4 + n_base], refs[4 + n_base : -1], refs[-1]
    quarter = pieces[0].shape[0]
    total = None
    for term, piece in enumerate(pieces):
        slot, side = numbers[1 + 2 * term], numbers[2 + 2 * term]
        head = heads[3][...]
        for other in (2, 1, 0):
            head = jnp.where(slot == other, heads[other][...], head)
        head = jnp.where(side == 0, head[:, :quarter], head[:, quarter:])
        product = times(head, piece[...])
        total = product if total is None else total + product
    for term in base:
        total = total + term[...]
    out[...] = total.astype(out.dtype)


def kept_sums(flags, grad_0, grad_1, there, *refs):
    pieces, outs = refs[:8], refs[8:]
    flag = flags[0] != 0
    for number, out in enumerate(outs):
        early_0, early_1, late_0, late_1 = pieces[4 * number : 4 * number + 4]
        total = times_rows(grad_0[...], jnp.where(flag, early_0[...], late_0[...]))
        total = total + times_rows(grad_1[...], jnp.where(flag, early_1[...], late_1[...]))
        if number == 0:
            total = total + there[...]
        out[...] = total.astype(out.dtype)


def keep(early, grads, there, pieces):
    tokens, width = grads[0].shape
    quarter = pieces[0][0][0].shape[0]
    tile = tokens // 3
    by_rows = lambda columns: pl.BlockSpec((tile, columns), lambda i: (i, 0))
    flat = [p for four in pieces for two in four for p in two]
    return pl.pallas_call(
        kept_sums,
        grid=(tokens // tile,),
        in_specs=[pl.BlockSpec(memory_space=pltpu.SMEM)]
        + [by_rows(width)] * 2
        + [by_rows(quarter)]
        + [pl.BlockSpec(p.shape, lambda i: (0, 0), pipeline_mode=pl.Buffered(1)) for p in flat],
        out_specs=[by_rows(quarter)] * 2,
        out_shape=[jax.ShapeDtypeStruct((tokens, quarter), d) for d in (jnp.bfloat16, jnp.float32)],
        compiler_params=pltpu.CompilerParams(
            dimension_semantics=("arbitrary",), vmem_limit_bytes=60 * 1024 * 1024
        ),
        cost_estimate=pl.CostEstimate(flops=1000, bytes_accessed=1000, transcendentals=0),
    )(early.astype(jnp.int32).reshape(1), *grads, there, *flat)


def forward_sum(numbers, heads, base, pieces, dtype):
    tokens, width = heads[0].shape
    tile = tokens // 3
    by_rows = pl.BlockSpec((tile, width), lambda i, _: (i, 0))
    spec = pltpu.PrefetchScalarGridSpec(
        num_scalar_prefetch=1,
        grid=(tokens // tile,),
        in_specs=[pl.BlockSpec((tile, width // 2), lambda i, numbers: (i, numbers[0]))] * 4
        + [by_rows] * len(base)
        + [pl.BlockSpec(p.shape, lambda i, _: (0, 0), pipeline_mode=pl.Buffered(1)) for p in pieces],
        out_specs=by_rows,
    )
    return pl.pallas_call(
        functools.partial(sum_of_products, len(base)),
        grid_spec=spec,
        out_shape=jax.ShapeDtypeStruct((tokens, width), dtype),
        compiler_params=pltpu.CompilerParams(
            dimension_semantics=("arbitrary",), vmem_limit_bytes=60 * 1024 * 1024
        ),
        cost_estimate=pl.CostEstimate(flops=1000, bytes_accessed=1000, transcendentals=0),
    )(numbers, *heads, *base, *pieces)


INWARD = [(0, 1), (3, 2)]
MIDDLE = [(1, 2), (2, 1)]
OUTWARD = [(1, 0), (2, 3)]
BOTH = INWARD + OUTWARD


def grid_4(head_out, out_grad, proj_weight):
    group = lax.axis_index("g")
    plane = lax.axis_index("a")
    chip = lax.axis_index("b")
    core = lax.axis_index("k")
    heads, grad_0, weight = head_out[0], out_grad[0], proj_weight[0]
    tokens, width = heads.shape
    half, quarter = width // 2, width // 4
    is_mid = (plane == 1) | (plane == 2)
    early = plane // 2 != chip

    def weight_rows(block, of_core, of_group):
        return lax.dynamic_slice_in_dim(block, of_core * half + of_group * quarter, quarter, 0)

    def sums(early_pieces, late_pieces):
        slot_0, slot_1 = (pick(early, e, l) for e, l in zip(early_pieces, late_pieces))
        return times_rows(grad_0, slot_0) + times_rows(grad_1, slot_1)

    low = plane < 2
    near, far, far_next = plane ^ 1, pick(low, 2, 1), pick(low, 3, 0)

    def numbers_of(rows):
        numbers = [core]
        for row in rows:
            slot = 2 * (row // 2 != chip) + ((row & 1) != core)
            numbers += [slot, group, slot, 1 - group]
        return jnp.stack(numbers).astype(jnp.int32)

    numbers_1 = numbers_of([plane, near, pick(early, far, far_next), pick(early, far_next, far)])
    numbers_0 = numbers_of([plane, pick(early, near, far), pick(early, far, far_next), pick(early, far_next, near)])

    mine_0 = weight_rows(weight, core, group)
    middle_0 = send(mine_0, MIDDLE)
    mine_1 = swap(weight_rows(after(weight, mine_0), 1 - core, group), "k")
    head_y = swap(heads, "b")
    near_1 = send(mine_1, BOTH)
    middle_1 = send(after(mine_1, near_1, middle_0), MIDDLE)
    grad_1 = swap(grad_0, "k")
    x_1 = swap(near_1, "g")
    ahead = is_mid & jnp.logical_not(early)
    mid_2 = pick(ahead, middle_0, mine_0)
    out_2 = send(after(mid_2, near_1), BOTH)
    cross_1 = send(after(near_1, middle_1), MIDDLE)
    mid_3 = pick(early, middle_0, after(middle_1, mid_2))
    out_3 = send(after(mid_3, out_2, x_1), OUTWARD)
    at_2 = pick(ahead, middle_0, after(out_2, mid_3))
    x_2 = swap(after(at_2, x_1, grad_1), "g")
    cross_0 = send(after(out_2, cross_1), MIDDLE)
    late_weight = after(weight, x_1)
    other_0 = weight_rows(late_weight, core, 1 - group)
    other_1 = swap(weight_rows(late_weight, 1 - core, 1 - group), "k")
    mid_4 = pick(early, middle_1, after(cross_1, at_2))
    out_4 = send(after(mid_4, out_3), OUTWARD)
    at_3 = pick(is_mid, mid_3, after(out_3, x_1, other_0, other_1, mid_4, head_y))
    due_1 = sums((mine_0, mine_1), (at_2, at_3))
    x_3 = swap(after(at_3, x_2, due_1), "g")

    there = swap(after(due_1, head_y), "b")
    due = sums((other_0, other_1), (x_2, x_3))
    first, due, numbers_0, numbers_1 = lax.optimization_barrier((there, due, numbers_0, numbers_1))
    there = swap(due, "b")
    mid_5 = pick(early, cross_1, after(cross_0, at_3))
    out_5 = send(after(mid_5, out_4), OUTWARD)
    at_4 = pick(is_mid, mid_4, after(out_4, x_2, mid_5))
    x_4 = swap(after(at_4, x_3), "g")
    late_6 = pick(early, cross_0, after(mine_0, at_4))
    out_6 = send(after(late_6, out_5), OUTWARD)
    at_5 = pick(is_mid, mid_5, after(out_5, x_3, late_6))
    x_5 = swap(after(at_5, x_4), "g")

    head_1, head_3 = swap(after(heads, x_2), "k"), swap(after(head_y, x_2), "k")
    due = sums((at_2, near_1), (at_5, at_4))
    kept_1 = sums(*after(((at_3, at_4), (mine_0, mine_1)), first))
    kept_2 = sums((x_3, x_4), (other_0, other_1))
    second, due, head_1, head_3, kept_1, kept_2 = lax.optimization_barrier(
        (there, due, head_1, head_3, kept_1, kept_2)
    )
    there = swap(due, "b")
    at_6 = pick(is_mid, pick(early, cross_0, out_2), after(out_6, second))
    x_6 = swap(after(at_6, x_5), "g")

    head_all = [heads, head_1, head_y, head_3]

    pieces_1 = [mine_1, other_1, near_1, x_1, at_4, x_4, pick(early, at_5, at_3), pick(early, x_5, x_3)]
    pieces_0 = [mine_0, other_0, at_2, x_2, pick(early, at_3, at_5), pick(early, x_3, x_5), at_6]
    total_1 = forward_sum(numbers_1, head_all, [], pieces_1, jnp.float32)
    due = sums((x_2, x_1), (x_5, x_4))
    third, due, total_1, x_6 = lax.optimization_barrier((there, due, total_1, x_6))
    there = swap(due, "b")
    other_part = swap(total_1, "k")
    projected = forward_sum(numbers_0, head_all, [other_part], pieces_0 + [x_6], jnp.bfloat16)

    done = [(k + t).astype(jnp.bfloat16) for k, t in ((kept_1, first), (kept_2, second))]
    last, kept = keep(
        early, [grad_0, grad_1], third, [((at_6, at_5), (at_6, near_1)), ((x_6, x_5), (x_6, x_1))]
    )
    done.append(last)
    first_mine = pick(early, plane // 2, plane & 1) == core
    here_z, got_z = pick(first_mine, done[0], done[2]), swap(pick(first_mine, done[2], done[0]), "k")
    head_grad = jnp.zeros_like(heads)
    for of_core, part in ((core, here_z), (1 - core, got_z)):
        head_grad = lax.dynamic_update_slice_in_dim(head_grad, part, of_core * half + group * quarter, 1)
    done, kept, projected, head_grad, there = lax.optimization_barrier((done, kept, projected, head_grad, there))
    done.append((kept + there).astype(jnp.bfloat16))
    here_x, got_x = pick(first_mine, done[1], done[3]), swap(pick(first_mine, done[3], done[1]), "k")
    for of_core, part in ((core, here_x), (1 - core, got_x)):
        head_grad = lax.dynamic_update_slice_in_dim(head_grad, part, of_core * half + (1 - group) * quarter, 1)
    return projected[None], head_grad[None]


def solution(mesh):
    n_group, n_row = mesh.shape["groups"], mesh.shape["row"]
    if (n_group, n_row) == (2, 16):
        grid = Mesh(mesh.devices.reshape(2, 4, 2, 2), ("g", "a", "b", "k"))
        tokens, whole = P(("a", "b", "k"), "g", None), P(("a", "b", "k"), None, None)
        body = grid_4
    else:
        grid = mesh
        tokens, whole = P("row", "groups", None), P("row", None, None)
        body = any_grid
    return jax.shard_map(
        body, mesh=grid, in_specs=(tokens, tokens, whole), out_specs=(tokens, tokens), check_vma=False
    )
```
